256 devices in a mesh: dp: 8 (over x_hi, y), tensor: 32 (over z, x_lo, core).
Axes of the slice: x: 4 (x_hi: 2, x_lo: 2; x = x_hi * 2 + x_lo), y: 4, z: 8, core: 2. Of those that a mesh axis runs over, the one named last changes fastest.
Arguments:
- tokens: bfloat16 [5120, 8192], P('dp', 'tensor'), may hold values from -6 to 6
- cotangent: bfloat16 [5120, 8192], P('dp', 'tensor'), may hold values from -6 to 6
- up_blocks: bfloat16 [6, 256, 32768], P(None, None, 'tensor'), may hold values from -0.15625 to 0.15625
- down_blocks: bfloat16 [6, 32768, 256], P(None, 'tensor'), may hold values from -0.078125 to 0.078125
- up_left: bfloat16 [8192, 256], P('tensor'), may hold values from -0.0625 to 0.0625
- up_right: bfloat16 [256, 32768], P(None, 'tensor'), may hold values from -0.375 to 0.375
- down_left: bfloat16 [32768, 256], P('tensor'), may hold values from -0.03125 to 0.03125
- down_right: bfloat16 [256, 8192], P(None, 'tensor'), may hold values from -0.375 to 0.375
- section_perm: int32 [5, 256], replicated, may hold values from 0 to 255, each once within a row
Outputs:
- output: bfloat16 [5120, 8192], P('dp', 'tensor')
- grad_tokens: bfloat16 [5120, 8192], P('dp', 'tensor')
- grad_up_blocks: float32 [6, 256, 32768], P(None, None, ('tensor', 'dp'))
- grad_down_blocks: float32 [6, 32768, 256], P(None, ('tensor', 'dp'))
- grad_up_left: float32 [8192, 256], P('tensor', 'dp')
- grad_up_right: float32 [256, 32768], P(None, ('tensor', 'dp'))
- grad_down_left: float32 [32768, 256], P(('tensor', 'dp'))
- grad_down_right: float32 [256, 8192], P('dp', 'tensor')
The draws below stay inside these ranges and needn't reach their ends.
Inputs may be any that keep to these rules, and one draw needn't show every extreme that they name: Each row of section_perm is a permutation of 0 to 255.
All inputs are finite; a program needn't handle non-finite values.
Results may differ from the reference program's by a relative error of at most 0.007.
Values may be sent and summed in bfloat16 or wider, within the bound.
No kernel may reach another device: no remote copies, remote signals or barrier semaphores. Data moves between devices by JAX's collectives and lax.ppermute only.
A program may use at most 192 MiB of HBM per device.

```python
import jax
import jax.numpy as jnp
from jax import lax

BLK = 256
SECTIONS = 5
D = 8192
H = 32768
R = 256
TOK_DEV = 640
TOKENS = 5120
N_DP = 8


def steps_of(stream_key, shape, cuts, smallest, high):
    gain, own = 1.0, jax.random.fold_in(stream_key, 6)
    for position, shards_of in cuts:
        steps = jnp.exp(jax.random.uniform(jax.random.fold_in(own, position), (shards_of,), jnp.float32, smallest / len(cuts), high / len(cuts)))
        gain = gain * jnp.repeat(steps, shape[position] // shards_of).reshape([-1 if axis == position else 1 for axis in range(len(shape))])
    return gain


def bell_draw(rng, extent, width, bound, pieces=(), kind=jnp.bfloat16):
    drawn = jax.random.normal(rng, extent, jnp.float32) * width
    if len(pieces) > 0:
        drawn = steps_of(rng, extent, pieces, -0.22, 0.18) * drawn
    return jnp.clip(drawn, min=-bound, max=bound).astype(kind)


def setup_inputs(seed: int = 0) -> dict:
    key_of = jax.random.split(jax.random.key(seed), 10)
    return {
        "tokens": bell_draw(key_of[0], (TOKENS, D), 1.0, 6.0, ((0, 8), (1, 32))),
        "cotangent": bell_draw(key_of[1], (TOKENS, D), 1.0, 6.0, ((0, 8), (1, 32))),
        "up_blocks": bell_draw(key_of[2], (SECTIONS + 1, BLK, H), ((SECTIONS + 1) * BLK) ** -0.5, 0.15625, ((2, 32),)),
        "down_blocks": bell_draw(key_of[3], (SECTIONS + 1, H, BLK), ((SECTIONS + 1) * H // (D // BLK)) ** -0.5, 0.078125, ((1, 32),)),
        "up_left": bell_draw(key_of[4], (D, R), D ** -0.5, 0.0625, ((0, 32),)),
        "up_right": bell_draw(key_of[5], (R, H), R ** -0.5, 0.375, ((1, 32),)),
        "down_left": bell_draw(key_of[6], (H, R), H ** -0.5, 0.03125, ((0, 32),)),
        "down_right": bell_draw(key_of[7], (R, D), R ** -0.5, 0.375, ((1, 32),)),
        "section_perm": jax.vmap(lambda own: jax.random.permutation(own, BLK))(jax.random.split(key_of[8], SECTIONS)).reshape((SECTIONS, BLK)).astype(jnp.int32),
    }


def gelu_tanh(value):
    return jax.nn.gelu(value, approximate=True)

def rounded(value):
    return lax.optimization_barrier(value.astype(jnp.bfloat16)).astype(jnp.float32)

def reference(tokens, cotangent, up_blocks, down_blocks, up_left, up_right, down_left, down_right, section_perm):
    f32 = jnp.float32
    bf16 = jnp.bfloat16
    nblk = D // BLK
    per_blk = H // nblk
    upf = up_blocks.astype(f32).reshape(SECTIONS + 1, BLK, nblk, per_blk)
    downf = down_blocks.astype(f32).reshape(SECTIONS + 1, nblk, per_blk, BLK)
    index = jnp.arange(nblk, dtype=jnp.int32)
    partners = [jnp.bitwise_xor(index, jnp.int32(1 << k)) for k in range(SECTIONS)]

    def one_group(carry, data):
        xg, dyg = data
        x3 = xg.astype(f32).reshape(TOK_DEV, nblk, BLK)
        moved = [jnp.take(x3[:, partners[k]], section_perm[k], axis=2) for k in range(SECTIONS)]
        low_in = jnp.dot(xg, up_left, preferred_element_type=f32).astype(bf16)
        pre = jnp.einsum('tmb,bmh->tmh', x3, upf[0])
        for k in range(SECTIONS):
            pre = pre + jnp.einsum('tmb,bmh->tmh', moved[k], upf[k + 1])
        pre = pre + jnp.dot(low_in, up_right, preferred_element_type=f32).reshape(TOK_DEV, nblk, per_blk)
        act = gelu_tanh(pre).astype(bf16)
        act2 = act.reshape(TOK_DEV, H)
        low_hidden = jnp.dot(act2, down_left, preferred_element_type=f32).astype(bf16)
        actf = act.astype(f32)
        result = jnp.einsum('tmh,mhb->tmb', actf, downf[0])
        for k in range(SECTIONS):
            piece = rounded(jnp.einsum('tmh,mhb->tmb', actf, downf[k + 1]))
            result = result + piece[:, partners[k]]
        result = result + jnp.dot(low_hidden, down_right, preferred_element_type=f32).reshape(TOK_DEV, nblk, BLK)
        out = result.reshape(TOK_DEV, D).astype(bf16)
        dy3 = dyg.astype(f32).reshape(TOK_DEV, nblk, BLK)
        dmoved = [dy3[:, partners[k]] for k in range(SECTIONS)]
        back_low = jnp.dot(dyg, down_right.T, preferred_element_type=f32).astype(bf16)
        dact = jnp.einsum('tmb,mhb->tmh', dy3, downf[0])
        for k in range(SECTIONS):
            dact = dact + jnp.einsum('tmb,mhb->tmh', dmoved[k], downf[k + 1])
        dact = dact + jnp.dot(back_low, down_left.T, preferred_element_type=f32).reshape(TOK_DEV, nblk, per_blk)
        dpre = jax.vjp(gelu_tanh, pre)[1](dact)[0].astype(bf16)
        dpre2 = dpre.reshape(TOK_DEV, H)
        back_in = jnp.dot(dpre2, up_right.T, preferred_element_type=f32).astype(bf16)
        dpref = dpre.astype(f32)
        back = jnp.einsum('tmh,bmh->tmb', dpref, upf[0])
        for k in range(SECTIONS):
            piece = rounded(jnp.einsum('tmh,bmh->tmb', dpref, upf[k + 1]))
            placed = jnp.zeros_like(piece).at[:, :, section_perm[k]].set(piece)
            back = back + placed[:, partners[k]]
        back = back + jnp.dot(back_in, up_left.T, preferred_element_type=f32).reshape(TOK_DEV, nblk, BLK)
        grad_x = back.reshape(TOK_DEV, D).astype(bf16)
        g_up = jnp.stack([jnp.einsum('tmb,tmh->bmh', x3, dpref)] + [jnp.einsum('tmb,tmh->bmh', moved[k], dpref) for k in range(SECTIONS)]).reshape(SECTIONS + 1, BLK, H)
        g_down = jnp.stack([jnp.einsum('tmh,tmb->mhb', actf, dy3)] + [jnp.einsum('tmh,tmb->mhb', actf, dmoved[k]) for k in range(SECTIONS)]).reshape(SECTIONS + 1, H, BLK)
        g_uleft = jnp.dot(xg.astype(f32).T, back_in.astype(f32))
        g_uright = jnp.dot(low_in.astype(f32).T, dpref.reshape(TOK_DEV, H))
        g_dleft = jnp.dot(actf.reshape(TOK_DEV, H).T, back_low.astype(f32))
        g_dright = jnp.dot(low_hidden.astype(f32).T, dyg.astype(f32))
        terms = (g_up, g_down, g_uleft, g_uright, g_dleft, g_dright)
        carry = tuple((total + term for total, term in zip(carry, terms)))
        return (carry, (out, grad_x))
    init = (jnp.zeros((SECTIONS + 1, BLK, H), f32), jnp.zeros((SECTIONS + 1, H, BLK), f32), jnp.zeros((D, R), f32), jnp.zeros((R, H), f32), jnp.zeros((H, R), f32), jnp.zeros((R, D), f32))
    groups = (tokens.reshape(N_DP, TOK_DEV, D), cotangent.reshape(N_DP, TOK_DEV, D))
    totals, stacked = lax.scan(one_group, init, groups)
    output = stacked[0].reshape(TOKENS, D)
    grad_tokens = stacked[1].reshape(TOKENS, D)
    return (output, grad_tokens, totals[0], totals[1], totals[2], totals[3], totals[4], totals[5])
```

```python
import jax
import jax.numpy as jnp
from jax import lax
from jax.sharding import PartitionSpec as P

BLK = 256
F32 = jnp.float32
BF16 = jnp.bfloat16


def swap(value, mask):
    pairs = [(source, source ^ mask) for source in range(lax.axis_size("tensor"))]
    return lax.ppermute(value, "tensor", pairs)


def last_dot(left, right):
    return lax.dot_general(
        left, right, (((1,), (1,)), ((), ())), preferred_element_type=F32
    )


def first_dot(left, right):
    return lax.dot_general(
        left, right, (((0,), (0,)), ((), ())), preferred_element_type=F32
    )


def dot(left, right):
    return jnp.dot(left, right, preferred_element_type=F32)


def halve(value, bit, mask, axis, wire):
    low, high = jnp.split(value, 2, axis)
    kept = jnp.where(bit, high, low)
    sent = jnp.where(bit, low, high).astype(wire)
    return kept + swap(sent, mask).astype(F32)


def double(value, bit, mask, axis):
    other = swap(value, mask)
    return jnp.where(
        bit,
        jnp.concatenate([other, value], axis),
        jnp.concatenate([value, other], axis),
    )


def sum_pair(first, second, bits):
    core, near, z_one, z_two, z_four = bits
    kept = jnp.where(core, second, first)
    sent = jnp.where(core, first, second).astype(BF16)
    value = kept + swap(sent, 1).astype(F32)
    value = halve(value, near, 2, 0, BF16)
    value = halve(value, z_one, 4, 0, F32)
    value = halve(value, z_two, 8, 0, F32)
    value = halve(value, z_four, 16, 1, F32)
    value = value.astype(BF16)
    value = double(value, z_four, 16, 1)
    value = double(value, z_two, 8, 0)
    value = double(value, z_one, 4, 0)
    value = double(value, near, 2, 0)
    other = swap(value, 1)
    return jnp.where(core, other, value), jnp.where(core, value, other)


def to_dp(value, pairs):
    return lax.ppermute(value, "dp", pairs)


def y_sum(chunks, y):
    total = lax.dynamic_index_in_dim(chunks, y, 0, False)
    for step in (2, 1, 3):
        sent = lax.dynamic_index_in_dim(chunks, (y + step) % 4, 0, False).astype(BF16)
        pairs = [(i, (i // 4) * 4 + (i + step) % 4) for i in range(8)]
        total = total + to_dp(sent, pairs).astype(F32)
    return total


def x_sum(halves, x_hi):
    kept = lax.dynamic_index_in_dim(halves, x_hi, 0, False)
    sent = lax.dynamic_index_in_dim(halves, 1 - x_hi, 0, False).astype(BF16)
    return kept + to_dp(sent, [(i, i ^ 4) for i in range(8)]).astype(F32)


def gelu_both(pre):
    scale = 0.7978845608028654
    cubic = 0.044715
    square = pre * pre
    inner = jnp.tanh(scale * pre * (1.0 + cubic * square))
    half = 0.5 * (1.0 + inner)
    slope = half + 0.5 * pre * (1.0 - inner * inner) * (
        scale * (1.0 + 3.0 * cubic * square)
    )
    return pre * half, slope


def local(
    tokens,
    cotangent,
    up_blocks,
    down_blocks,
    up_left,
    up_right,
    down_left,
    down_right,
    section_perm,
):
    sections = section_perm.shape[0]
    me = lax.axis_index("tensor")
    dp = lax.axis_index("dp")
    x_hi, y = dp // 4, dp % 4
    bits = [(me >> k) & 1 == 1 for k in range(5)]

    x_in, c_in = [None] * 5, [None] * 5
    x_in[3] = swap(tokens, 8)
    c_in[3] = swap(cotangent, 8)
    both = jnp.concatenate([tokens, cotangent], 1)
    for k in (0, 1, 2):
        got = swap(both, 2**k)
        x_in[k], c_in[k] = got[:, :BLK], got[:, BLK:]
    x_in[4] = swap(x_in[3], 24)
    c_in[4] = swap(c_in[3], 24)
    low_in, back_low = sum_pair(
        dot(tokens, up_left), last_dot(cotangent, down_right), bits
    )

    order = (
        jnp.arange(BLK, dtype=section_perm.dtype)[None, :, None]
        == section_perm[:, None, :]
    ).astype(BF16)
    ups = [up_blocks[0]] + [
        dot(order[k], up_blocks[k + 1]).astype(BF16) for k in range(sections)
    ]
    moved = [tokens] + [dot(x_in[k], order[k]).astype(BF16) for k in range(sections)]
    xs = [tokens] + x_in
    cs = [cotangent] + c_in

    pre = dot(low_in, up_right)
    for k in range(sections + 1):
        pre = pre + dot(xs[k], ups[k])
    dact = last_dot(back_low, down_left)
    for k in range(sections + 1):
        dact = dact + last_dot(cs[k], down_blocks[k])
    act, slope = gelu_both(pre)
    act = act.astype(BF16)
    dpre = (dact * slope).astype(BF16)

    part = [dot(act, down_blocks[k]) for k in range(sections + 1)]
    back = [last_dot(dpre, ups[k]) for k in range(sections + 1)]
    part4 = swap(part[5].astype(BF16), 24).astype(F32) + part[4]
    back4 = swap(back[5].astype(BF16), 24).astype(F32) + back[4]
    part4 = swap(part4.astype(BF16), 8).astype(F32)
    back4 = swap(back4.astype(BF16), 8).astype(F32)
    result = part[0] + part4
    grad = back[0] + back4
    for k in (0, 1, 2):
        got = swap(
            jnp.concatenate([part[k + 1].astype(BF16), back[k + 1].astype(BF16)], 1),
            2**k,
        )
        result = result + got[:, :BLK].astype(F32)
        grad = grad + got[:, BLK:].astype(F32)
    low_hidden, back_in = sum_pair(
        dot(act, down_left), last_dot(dpre, up_right), bits
    )
    output = (result + dot(low_hidden, down_right)).astype(BF16)
    grad_tokens = (grad + last_dot(back_in, up_left)).astype(BF16)

    g_down = jnp.stack(
        [first_dot(act, c) for c in cs] + [first_dot(act, back_low)]
    ).reshape(7, 2, 4, 128, BLK)
    g_down = x_sum(g_down.transpose(1, 2, 0, 3, 4), x_hi)
    g_down = y_sum(g_down, y)
    g_up = first_dot(jnp.concatenate(moved + [low_in], 1), dpre).reshape(
        7, BLK, 2, 4, 128
    )
    g_up = y_sum(g_up.transpose(3, 2, 0, 1, 4), y)
    g_up = x_sum(g_up, x_hi)
    g_small = jnp.stack(
        [first_dot(back_in, tokens), first_dot(low_hidden, cotangent)]
    ).reshape(2, 2, 4, 32, BLK)
    g_small = y_sum(g_small.transpose(2, 1, 0, 3, 4), y)
    g_small = x_sum(g_small, x_hi)
    return (
        output,
        grad_tokens,
        g_up[:6],
        g_down[:6],
        g_small[0].T,
        g_up[6],
        g_down[6],
        g_small[1],
    )


def solution(mesh):
    placed = (
        P("dp", "tensor"),
        P("dp", "tensor"),
        P(None, None, "tensor"),
        P(None, "tensor", None),
        P("tensor", None),
        P(None, "tensor"),
        P("tensor", None),
        P(None, "tensor"),
        P(),
    )
    return jax.shard_map(
        local,
        mesh=mesh,
        in_specs=placed,
        out_specs=(
            P("dp", "tensor"),
            P("dp", "tensor"),
            P(None, None, ("tensor", "dp")),
            P(None, ("tensor", "dp"), None),
            P("tensor", "dp"),
            P(None, ("tensor", "dp")),
            P(("tensor", "dp"), None),
            P("dp", "tensor"),
        ),
        check_vma=False,
    )
```

```python
import jax
import jax.numpy as jnp
from jax import lax
from jax.experimental import pallas as pl
from jax.experimental.pallas import tpu as pltpu
from jax.sharding import PartitionSpec as P

BLK = 256
F32 = jnp.float32
BF16 = jnp.bfloat16


def swap(value, mask):
    pairs = [(source, source ^ mask) for source in range(lax.axis_size("tensor"))]
    return lax.ppermute(value, "tensor", pairs)


def last_dot(left, right):
    return lax.dot_general(
        left, right, (((1,), (1,)), ((), ())), preferred_element_type=F32
    )


def first_dot(left, right):
    return lax.dot_general(
        left, right, (((0,), (0,)), ((), ())), preferred_element_type=F32
    )


def dot(left, right):
    return jnp.dot(left, right, preferred_element_type=F32)


def after(value, *earlier):
    return lax.optimization_barrier((value, *earlier))[0]


def halve(value, bit, mask):
    low, high = jnp.split(value, 2, 0)
    return jnp.where(bit, high, low) + swap(jnp.where(bit, low, high), mask)


def double(value, bit, mask):
    other = swap(value, mask)
    return jnp.where(
        bit,
        jnp.concatenate([other, value], 0),
        jnp.concatenate([value, other], 0),
    )


def both_halves(value):
    size = lax.axis_size("tensor")
    groups = [list(range(i, i + 4)) for i in range(0, size, 4)]
    return lax.all_gather(value, "tensor", axis_index_groups=groups)


def joined(lows, index):
    return jnp.concatenate([lows[index], lows[index + 2]], 0)


def to_dp(value, pairs):
    return lax.ppermute(value, "dp", pairs)


def y_pairs(step):
    return [(i, (i // 4) * 4 + (i + step) % 4) for i in range(8)]


X_PAIRS = [(i, i ^ 4) for i in range(8)]
VMEM = pl.BlockSpec(memory_space=pltpu.VMEM)
SMEM = pl.BlockSpec(memory_space=pltpu.SMEM)


def call(kernel, outs, flops, args):
    shapes = [jax.ShapeDtypeStruct(shape, kind) for shape, kind in outs]
    moved = sum(x.size * x.dtype.itemsize for x in (*args, *shapes))
    return pl.pallas_call(
        kernel,
        out_shape=shapes,
        in_specs=[SMEM if x.dtype == jnp.int32 else VMEM for x in args],
        out_specs=[VMEM] * len(shapes),
        compiler_params=pltpu.CompilerParams(vmem_limit_bytes=10 * 2**20),
        cost_estimate=pl.CostEstimate(
            flops=flops, bytes_accessed=moved, transcendentals=0
        ),
    )(*args)


def quarters(bits, first, second, outs):
    rows = first.shape[0] // 2
    core, near = bits[0] == 1, bits[1] == 1
    mine, other = jnp.where(core, second, first), jnp.where(core, first, second)
    kept, to_core, to_near, to_far = outs
    kept[...] = jnp.where(near, mine[rows:], mine[:rows])
    to_core[...] = jnp.where(near, other[rows:], other[:rows])
    to_near[...] = jnp.where(near, mine[:rows], mine[rows:]).astype(BF16)
    to_far[...] = jnp.where(near, other[:rows], other[rows:]).astype(BF16)


def low_kernel(bits, tokens, cotangent, up_left, down_right, *outs):
    first = dot(tokens[...], up_left[...])
    second = last_dot(cotangent[...], down_right[...])
    quarters(bits, first, second, outs)


def middle_kernel(
    bits, x_0, b_0, b_1, x_2, x_3, x_4, c_0, c_2, c_3, c_4, lows,
    up_0, up_1, up_2, up_3, up_4, up_5, up_right, down, down_left,
    act, dpre, low_in, back_low, kept, fold_out, fold_back, far_out, far_back, send_0, send_1, send_2, *outs,
):
    ups = (up_0, up_1, up_2, up_3, up_4, up_5)
    left, right = slice(0, BLK), slice(BLK, 2 * BLK)
    low_in[...] = joined(lows, 0)
    back_low[...] = joined(lows, 1)
    for j in range(0, 1024, BLK):
        cols = slice(j, j + BLK)
        pre = dot(low_in[...], up_right[:, cols])
        dact = last_dot(back_low[...], down_left[cols, :])
        for k, (x, c) in enumerate((
            (x_0[...], c_0[...]), (b_0[:, left], b_0[:, right]), (b_1[:, left], b_1[:, right]),
            (x_2[...], c_2[...]), (x_3[...], c_3[...]), (x_4[...], c_4[...]),
        )):
            pre = pre + dot(x, ups[k][:, cols])
            dact = dact + last_dot(c, down[k, cols, :])
        value, slope = gelu_both(pre)
        act[:, cols] = value.astype(BF16)
        dpre[:, cols] = (dact * slope).astype(BF16)
    quarters(bits, dot(act[...], down_left[...]), last_dot(dpre[...], up_right[...]), outs)
    for out, back, k in ((far_out, far_back, 5), (fold_out, fold_back, 4)):
        out[...] = dot(act[...], down[k]).astype(out.dtype)
        back[...] = last_dot(dpre[...], ups[k][...]).astype(back.dtype)
    for target, k in ((send_1, 2), (send_2, 3), (send_0, 1), (kept, 0)):
        target[:, left] = dot(act[...], down[k]).astype(target.dtype)
        target[:, right] = last_dot(dpre[...], ups[k][...]).astype(target.dtype)


def weight_kernel(
    steps, act, dpre, c_4, low_in, back_low, c, b_0, b_1, c_2, c_3, m_0, m_1, m_2, m_3, m_4, m_5,
    down_sent, up_1, up_3, up_2, up_kept, down_kept,
):
    cut = slice(BLK, 2 * BLK)
    for n, out in ((4, down_sent), (5, down_kept)):
        left = act[:, pl.ds(pl.multiple_of(steps[n] * 512, 512), 512)]
        rights = (c[...], b_0[:, cut], b_1[:, cut], c_2[...], c_3[...], c_4[...], back_low[...])
        for k, right in enumerate(rights):
            out[k] = first_dot(left, right).astype(out.dtype)
    for n, out in enumerate((up_1, up_3, up_2, up_kept)):
        begin = pl.multiple_of(steps[n] * 128, 128)
        right = jnp.concatenate(
            [dpre[:, pl.ds(begin, 128)], dpre[:, pl.ds(begin + 512, 128)]], 1
        )
        for k, left in enumerate((m_0, m_1, m_2, m_3, m_4, m_5, low_in)):
            out[k * BLK : (k + 1) * BLK] = first_dot(left[...], right).astype(out.dtype)


def low_terms_kernel(lows, kept, got_0, down_right, up_left, tokens, cotangent, total, small):
    low_hidden, back_in = joined(lows, 0), joined(lows, 1)
    left = first_dot(back_in, tokens[...]).astype(BF16)
    right = first_dot(low_hidden, cotangent[...]).astype(BF16)
    for n in range(8):
        rows = slice(32 * n, 32 * n + 32)
        small[n, :, :BLK] = left[rows]
        small[n, :, BLK:] = right[rows]
    for cols, term in (
        (slice(0, BLK), dot(low_hidden, down_right[...])),
        (slice(BLK, 2 * BLK), last_dot(back_in, up_left[...])),
    ):
        total[:, cols] = kept[:, cols] + term + got_0[:, cols].astype(F32)


def last_kernel(total, fold_out, fold_back, got_1, got_2, output, grad):
    for target, cols, fold in (
        (output, slice(0, BLK), fold_out),
        (grad, slice(BLK, 2 * BLK), fold_back),
    ):
        terms = [ref[:, cols].astype(F32) for ref in (got_1, got_2)]
        target[...] = (total[:, cols] + fold[...].astype(F32) + terms[0] + terms[1]).astype(BF16)


def part_of(value, index, size, axis):
    return lax.dynamic_slice_in_dim(value, index * size, size, axis)


def gelu_both(pre):
    scale = 0.7978845608028654
    cubic = 0.044715
    square = pre * pre
    inner = jnp.tanh(scale * pre * (1.0 + cubic * square))
    half = 0.5 * (1.0 + inner)
    slope = half + 0.5 * pre * (1.0 - inner * inner) * (
        scale * (1.0 + 3.0 * cubic * square)
    )
    return pre * half, slope


def local(
    tokens,
    cotangent,
    up_blocks,
    down_blocks,
    up_left,
    up_right,
    down_left,
    down_right,
    section_perm,
):
    sections = section_perm.shape[0]
    me = lax.axis_index("tensor")
    dp = lax.axis_index("dp")
    x_hi, y = dp // 4, dp % 4
    bits = [(me >> k) & 1 == 1 for k in range(5)]

    pair_bits = jnp.stack([me & 1, (me >> 1) & 1]).astype(jnp.int32)
    quad = (me >> 2) & 3
    rows = tokens.shape[0]
    work = 2 * rows * BLK * 1024
    wide, pair, block, half = (rows, 1024), (rows, 2 * BLK), (rows, BLK), (rows // 2, BLK)
    part = rows // 8
    split = [(half, F32)] * 2 + [(half, BF16)] * 2

    order = (
        jnp.arange(BLK, dtype=section_perm.dtype)[None, :, None]
        == section_perm[:, None, :]
    ).astype(BF16)
    ups = [
        dot(order[k], up_blocks[k + 1]).astype(BF16) for k in range(sections)
    ]

    x_3 = swap(tokens, 8)
    x_2 = swap(tokens, 4)
    kept, to_core, to_near, to_far = call(
        low_kernel, split, work // 2, (pair_bits, tokens, cotangent, up_left, down_right)
    )
    both = jnp.concatenate([after(tokens, kept), cotangent], 1)
    value = kept + swap(to_core, 1) + swap(to_near, 2).astype(F32) + swap(to_far, 3).astype(F32)
    value, x_3, x_2, both, *ups = lax.optimization_barrier((value, x_3, x_2, both, *ups))
    c_3 = swap(after(cotangent, value), 8)
    x_4 = swap(x_3, 24)
    pieces = [swap(part_of(value, quad ^ d, part, 0), 4 * d) for d in (1, 2, 3)]
    value = part_of(value, quad, part, 0) + sum(pieces)
    value, both = lax.optimization_barrier((value, both))
    got_1 = swap(both, 2)
    got_0 = swap(both, 1)
    value = (value + swap(value, 16)).astype(BF16)
    value, x_4, c_3, got_0, got_1 = lax.optimization_barrier((value, x_4, c_3, got_0, got_1))
    c_4 = swap(c_3, 24)
    c_2 = swap(after(cotangent, value), 4)
    pieces = [value] + [swap(value, 4 * d) for d in (1, 2, 3)]
    ordered = []
    for j in range(4):
        one = [jnp.where(bits[2], pieces[d ^ 1], pieces[d]) for d in range(4)]
        ordered.append(jnp.where(bits[3], one[j ^ 2], one[j]))
    value = jnp.concatenate(ordered, 0)
    lows = both_halves(value)
    x_in = [got_0[:, :BLK], got_1[:, :BLK], x_2, x_3, x_4]
    ups = [up_blocks[0]] + ups
    moved = [tokens] + [dot(x_in[k], order[k]).astype(BF16) for k in range(sections)]
    c_4 = after(c_4, *moved[1:])
    (
        act, dpre, low_in, back_low, kept, fold_out, fold_back, far_out, far_back, send_0, send_1, send_2,
        low_kept, to_core, to_near, to_far,
    ) = call(
        middle_kernel,
        [(wide, BF16)] * 2 + [(block, BF16)] * 2 + [(pair, F32)] + [(block, F32)] * 2 + [(block, BF16)] * 2
        + [(pair, BF16)] * 3 + split,
        28 * work,
        (
            pair_bits, tokens, got_0, got_1, x_2, x_3, x_4, cotangent, c_2, c_3, c_4, lows,
            *ups, up_right, down_blocks, down_left,
        ),
    )

    value = low_kept + swap(to_core, 1) + swap(to_near, 2).astype(F32) + swap(to_far, 3).astype(F32)
    far_out = swap(far_out, 24)
    steps = jnp.stack([(y + 1) % 4, (y + 3) % 4, (y + 2) % 4, y, 1 - x_hi, x_hi]).astype(jnp.int32)
    down_half, up_quarter = (7, 512, BLK), (7 * BLK, BLK)
    down_sent, up_1, up_3, up_2, g_up, down_kept = call(
        weight_kernel,
        [(down_half, BF16)] + [(up_quarter, BF16)] * 3 + [(up_quarter, F32), (down_half, F32)],
        14 * work,
        (steps, act, dpre, c_4, low_in, back_low, cotangent, got_0, got_1, c_2, c_3, *moved),
    )
    value, far_out, down_sent, up_1, up_3, up_2, g_up, down_kept = lax.optimization_barrier(
        (value, far_out, down_sent, up_1, up_3, up_2, g_up, down_kept)
    )
    got_y1, got_y3 = to_dp(up_1, y_pairs(1)), to_dp(up_3, y_pairs(3))
    got_x = to_dp(down_sent, X_PAIRS)
    got_0 = swap(after(send_0, value), 1)
    fold_out = (fold_out + far_out.astype(F32)).astype(BF16)
    value = halve(value, bits[2], 4)
    value = halve(value, bits[3], 8)
    value, fold_out, got_0 = lax.optimization_barrier((value, fold_out, got_0))
    value = (value + swap(value, 16)).astype(BF16)
    value, got_y1, got_y3 = lax.optimization_barrier((value, got_y1, got_y3))
    got_y2 = to_dp(after(up_2, value), y_pairs(2))
    far_back = swap(after(far_back, value), 24)
    fold_out = swap(after(fold_out, value), 8)
    value = double(value, bits[3], 8)
    value = double(value, bits[2], 4)
    value, got_y2, got_x, far_back, fold_out = lax.optimization_barrier(
        (value, got_y2, got_x, far_back, fold_out)
    )
    fold_back = swap((fold_back + far_back.astype(F32)).astype(BF16), 8)
    got_1 = swap(after(send_1, value), 2)
    g_down = down_kept + got_x.astype(F32)
    down_kept = part_of(g_down, y, 128, 1)
    down_sent = [part_of(g_down, (y + step) % 4, 128, 1).astype(BF16) for step in (1, 3, 2)]
    down_got = [to_dp(down_sent[0], y_pairs(1)), to_dp(down_sent[1], y_pairs(3))]
    value, sent_2 = lax.optimization_barrier((value, down_sent[2]))
    lows = both_halves(value)
    lows, fold_back, down_got[0], down_got[1], sent_2, send_2, g_up = lax.optimization_barrier(
        (lows, fold_back, *down_got, sent_2, send_2, g_up)
    )
    total, small = call(
        low_terms_kernel, [(pair, F32), ((8, 32, 2 * BLK), BF16)], work,
        (lows, kept, got_0, down_right, up_left, tokens, cotangent),
    )
    small = lax.all_to_all(small, "dp", 0, 0, tiled=True).astype(F32).sum(0)
    got_2 = swap(send_2, 4)
    down_got.append(to_dp(sent_2, y_pairs(2)))
    g_up = g_up + got_y1.astype(F32) + got_y3.astype(F32) + got_y2.astype(F32)
    up_kept = jnp.where(x_hi == 1, g_up[:, 128:], g_up[:, :128])
    up_got = to_dp(jnp.where(x_hi == 1, g_up[:, :128], g_up[:, 128:]).astype(BF16), X_PAIRS)

    def down_sum(begin, end):
        return down_kept[begin:end] + sum(term[begin:end].astype(F32) for term in down_got)

    def up_sum(begin, end):
        cut = slice(begin * BLK, end * BLK)
        return up_kept[cut] + up_got[cut].astype(F32)

    sums = (up_sum(0, 6), down_sum(0, 6), up_sum(6, 7), down_sum(6, 7), small)
    fold_out, fold_back, got_2, total, *sums = lax.optimization_barrier((fold_out, fold_back, got_2, total, *sums))
    output, grad_tokens = call(
        last_kernel, [(block, BF16)] * 2, work // 8, (total, fold_out, fold_back, got_1, got_2)
    )
    return (
        output,
        grad_tokens,
        sums[0].reshape(6, BLK, 128),
        sums[1],
        sums[4][:, :BLK].T,
        sums[2],
        sums[3][0],
        sums[4][:, BLK:],
    )


def solution(mesh):
    placed = (
        P("dp", "tensor"),
        P("dp", "tensor"),
        P(None, None, "tensor"),
        P(None, "tensor", None),
        P("tensor", None),
        P(None, "tensor"),
        P("tensor", None),
        P(None, "tensor"),
        P(),
    )
    return jax.shard_map(
        local,
        mesh=mesh,
        in_specs=placed,
        out_specs=(
            P("dp", "tensor"),
            P("dp", "tensor"),
            P(None, None, ("tensor", "dp")),
            P(None, ("tensor", "dp"), None),
            P("tensor", "dp"),
            P(None, ("tensor", "dp")),
            P(("tensor", "dp"), None),
            P("dp", "tensor"),
        ),
        check_vma=False,
    )
```

```python
import jax
import jax.numpy as jnp
from jax import lax
from jax.experimental import pallas as pl
from jax.experimental.pallas import tpu as pltpu
from jax.sharding import PartitionSpec as P

BLK = 256
F32 = jnp.float32
BF16 = jnp.bfloat16


def swap(value, mask):
    pairs = [(source, source ^ mask) for source in range(lax.axis_size("tensor"))]
    return lax.ppermute(value, "tensor", pairs)


def last_dot(left, right):
    return lax.dot_general(
        left, right, (((1,), (1,)), ((), ())), preferred_element_type=F32
    )


def first_dot(left, right):
    return lax.dot_general(
        left, right, (((0,), (0,)), ((), ())), preferred_element_type=F32
    )


def dot(left, right):
    return jnp.dot(left, right, preferred_element_type=F32)


def after(value, *earlier):
    return lax.optimization_barrier((value, *earlier))[0]


def halve(value, bit, mask):
    low, high = jnp.split(value, 2, 0)
    return jnp.where(bit, high, low) + swap(jnp.where(bit, low, high), mask)


def double(value, bit, mask):
    other = swap(value, mask)
    return jnp.where(
        bit,
        jnp.concatenate([other, value], 0),
        jnp.concatenate([value, other], 0),
    )


def both_halves(value):
    size = lax.axis_size("tensor")
    groups = [list(range(i, i + 4)) for i in range(0, size, 4)]
    return lax.all_gather(value, "tensor", axis_index_groups=groups)


def joined(lows, index):
    return jnp.concatenate([lows[index], lows[index + 2]], 0)


def to_dp(value, pairs):
    return lax.ppermute(value, "dp", pairs)


def y_pairs(step):
    return [(i, (i // 4) * 4 + (i + step) % 4) for i in range(8)]


X_PAIRS = [(i, i ^ 4) for i in range(8)]
VMEM = pl.BlockSpec(memory_space=pltpu.VMEM)
SMEM = pl.BlockSpec(memory_space=pltpu.SMEM)


def call(kernel, outs, flops, args, limit=4):
    shapes = [jax.ShapeDtypeStruct(shape, kind) for shape, kind in outs]
    moved = sum(x.size * x.dtype.itemsize for x in (*args, *shapes))
    return pl.pallas_call(
        kernel,
        out_shape=shapes,
        in_specs=[SMEM if x.dtype == jnp.int32 else VMEM for x in args],
        out_specs=[VMEM] * len(shapes),
        compiler_params=pltpu.CompilerParams(vmem_limit_bytes=limit * 2**20),
        cost_estimate=pl.CostEstimate(
            flops=flops, bytes_accessed=moved, transcendentals=0
        ),
    )(*args)


def quarters(bits, first, second, outs):
    rows = first.shape[0] // 2
    core, near = bits[0] == 1, bits[1] == 1
    mine, other = jnp.where(core, second, first), jnp.where(core, first, second)
    kept, to_core, to_near, to_far = outs
    kept[...] = jnp.where(near, mine[rows:], mine[:rows])
    to_core[...] = jnp.where(near, other[rows:], other[:rows])
    to_near[...] = jnp.where(near, mine[:rows], mine[rows:]).astype(BF16)
    to_far[...] = jnp.where(near, other[:rows], other[rows:]).astype(BF16)


def low_kernel(bits, tokens, cotangent, up_left, down_right, *outs):
    first = dot(tokens[...], up_left[...])
    second = last_dot(cotangent[...], down_right[...])
    quarters(bits, first, second, outs)


def middle_kernel(
    bits, x_0, b_0, b_1, x_2, x_3, x_4, c_0, c_2, c_3, c_4, lows,
    up_0, up_1, up_2, up_3, up_4, up_5, up_right, down, down_left,
    act, dpre, low_in, back_low, kept, fold_out, fold_back, far_out, far_back, send_0, send_1, send_2, *outs,
):
    ups = (up_0, up_1, up_2, up_3, up_4, up_5)
    left, right = slice(0, BLK), slice(BLK, 2 * BLK)
    low_in[...] = joined(lows, 0)
    back_low[...] = joined(lows, 1)
    for j in range(0, 1024, BLK):
        cols = slice(j, j + BLK)
        pre = dot(low_in[...], up_right[:, cols])
        dact = last_dot(back_low[...], down_left[cols, :])
        for k, (x, c) in enumerate((
            (x_0[...], c_0[...]), (b_0[:, left], b_0[:, right]), (b_1[:, left], b_1[:, right]),
            (x_2[...], c_2[...]), (x_3[...], c_3[...]), (x_4[...], c_4[...]),
        )):
            pre = pre + dot(x, ups[k][:, cols])
            dact = dact + last_dot(c, down[k, cols, :])
        value, slope = gelu_both(pre)
        act[:, cols] = value.astype(BF16)
        dpre[:, cols] = (dact * slope).astype(BF16)
    quarters(bits, dot(act[...], down_left[...]), last_dot(dpre[...], up_right[...]), outs)
    for out, back, k in ((far_out, far_back, 5), (fold_out, fold_back, 4)):
        out[...] = dot(act[...], down[k]).astype(out.dtype)
        back[...] = last_dot(dpre[...], ups[k][...]).astype(back.dtype)
    for target, k in ((send_1, 2), (send_2, 3), (send_0, 1), (kept, 0)):
        target[:, left] = dot(act[...], down[k]).astype(target.dtype)
        target[:, right] = last_dot(dpre[...], ups[k][...]).astype(target.dtype)


def weight_kernel(
    steps, act, dpre, c_4, low_in, back_low, c, b_0, b_1, c_2, c_3, m_0, m_1, m_2, m_3, m_4, m_5,
    down_sent, up_1, up_3, up_2, up_kept, down_kept,
):
    cut = slice(BLK, 2 * BLK)
    for n, out in ((4, down_sent), (5, down_kept)):
        left = act[:, pl.ds(pl.multiple_of(steps[n] * 512, 512), 512)]
        rights = (c[...], b_0[:, cut], b_1[:, cut], c_2[...], c_3[...], c_4[...], back_low[...])
        for k, right in enumerate(rights):
            out[k] = first_dot(left, right).astype(out.dtype)
    for n, out in enumerate((up_1, up_3, up_2, up_kept)):
        begin = pl.multiple_of(steps[n] * 128, 128)
        right = jnp.concatenate(
            [dpre[:, pl.ds(begin, 128)], dpre[:, pl.ds(begin + 512, 128)]], 1
        )
        for k, left in enumerate((m_0, m_1, m_2, m_3, m_4, m_5, low_in)):
            out[k * BLK : (k + 1) * BLK] = first_dot(left[...], right).astype(out.dtype)


def low_terms_kernel(bits, mine, other, kept, got_0, down_right, up_left, tokens, cotangent, total, small):
    core = bits[0] == 1
    low_hidden = jnp.where(core, other[...], mine[...])
    back_in = jnp.where(core, mine[...], other[...])
    left = first_dot(back_in, tokens[...]).astype(BF16)
    right = first_dot(low_hidden, cotangent[...]).astype(BF16)
    for n in range(8):
        rows = slice(32 * n, 32 * n + 32)
        small[n, :, :BLK] = left[rows]
        small[n, :, BLK:] = right[rows]
    for cols, term in (
        (slice(0, BLK), dot(low_hidden, down_right[...])),
        (slice(BLK, 2 * BLK), last_dot(back_in, up_left[...])),
    ):
        total[:, cols] = kept[:, cols] + term + got_0[:, cols].astype(F32)


def last_kernel(total, fold_out, fold_back, got_1, got_2, output, grad):
    for target, cols, fold in (
        (output, slice(0, BLK), fold_out),
        (grad, slice(BLK, 2 * BLK), fold_back),
    ):
        terms = [ref[:, cols].astype(F32) for ref in (got_1, got_2)]
        target[...] = (total[:, cols] + fold[...].astype(F32) + terms[0] + terms[1]).astype(BF16)


def part_of(value, index, size, axis):
    return lax.dynamic_slice_in_dim(value, index * size, size, axis)


def gelu_both(pre):
    scale = 0.7978845608028654
    cubic = 0.044715
    square = pre * pre
    inner = jnp.tanh(scale * pre * (1.0 + cubic * square))
    half = 0.5 * (1.0 + inner)
    slope = half + 0.5 * pre * (1.0 - inner * inner) * (
        scale * (1.0 + 3.0 * cubic * square)
    )
    return pre * half, slope


def local(
    tokens,
    cotangent,
    up_blocks,
    down_blocks,
    up_left,
    up_right,
    down_left,
    down_right,
    section_perm,
):
    sections = section_perm.shape[0]
    me = lax.axis_index("tensor")
    dp = lax.axis_index("dp")
    x_hi, y = dp // 4, dp % 4
    bits = [(me >> k) & 1 == 1 for k in range(5)]

    pair_bits = jnp.stack([me & 1, (me >> 1) & 1]).astype(jnp.int32)
    quad = (me >> 2) & 3
    rows = tokens.shape[0]
    work = 2 * rows * BLK * 1024
    wide, pair, block, half = (rows, 1024), (rows, 2 * BLK), (rows, BLK), (rows // 2, BLK)
    part = rows // 8
    split = [(half, F32)] * 2 + [(half, BF16)] * 2

    order = (
        jnp.arange(BLK, dtype=section_perm.dtype)[None, :, None]
        == section_perm[:, None, :]
    ).astype(BF16)
    ups = [
        dot(order[k], up_blocks[k + 1]).astype(BF16) for k in range(sections)
    ]

    x_3 = swap(tokens, 8)
    x_2 = swap(tokens, 4)
    kept, to_core, to_near, to_far = call(
        low_kernel, split, work // 2, (pair_bits, tokens, cotangent, up_left, down_right)
    )
    both = jnp.concatenate([after(tokens, kept), cotangent], 1)
    value = kept + swap(to_core, 1) + swap(to_near, 2).astype(F32) + swap(to_far, 3).astype(F32)
    value, x_3, x_2, both, *ups = lax.optimization_barrier((value, x_3, x_2, both, *ups))
    c_3 = swap(after(cotangent, value), 8)
    x_4 = swap(x_3, 24)
    pieces = [swap(part_of(value, quad ^ d, part, 0), 4 * d) for d in (1, 2, 3)]
    value = part_of(value, quad, part, 0) + sum(pieces)
    value, both = lax.optimization_barrier((value, both))
    got_1 = swap(both, 2)
    got_0 = swap(both, 1)
    value = (value + swap(value, 16)).astype(BF16)
    value, x_4, c_3, got_0, got_1 = lax.optimization_barrier((value, x_4, c_3, got_0, got_1))
    c_4 = swap(c_3, 24)
    c_2 = swap(after(cotangent, value), 4)
    pieces = [value] + [swap(value, 4 * d) for d in (1, 2, 3)]
    ordered = []
    for j in range(4):
        one = [jnp.where(bits[2], pieces[d ^ 1], pieces[d]) for d in range(4)]
        ordered.append(jnp.where(bits[3], one[j ^ 2], one[j]))
    value = jnp.concatenate(ordered, 0)
    lows = both_halves(value)
    x_in = [got_0[:, :BLK], got_1[:, :BLK], x_2, x_3, x_4]
    ups = [up_blocks[0]] + ups
    moved = [tokens] + [dot(x_in[k], order[k]).astype(BF16) for k in range(sections)]
    c_4 = after(c_4, *moved[1:])
    (
        act, dpre, low_in, back_low, kept, fold_out, fold_back, far_out, far_back, send_0, send_1, send_2,
        low_kept, to_core, to_near, to_far,
    ) = call(
        middle_kernel,
        [(wide, BF16)] * 2 + [(block, BF16)] * 2 + [(pair, F32)] + [(block, F32)] * 2 + [(block, BF16)] * 2
        + [(pair, BF16)] * 3 + split,
        28 * work,
        (
            pair_bits, tokens, got_0, got_1, x_2, x_3, x_4, cotangent, c_2, c_3, c_4, lows,
            *ups, up_right, down_blocks, down_left,
        ),
        8,
    )

    from_core = swap(to_core, 1)
    value = low_kept + from_core + swap(to_near, 2).astype(F32) + swap(to_far, 3).astype(F32)
    far_out = swap(far_out, 24)
    steps = jnp.stack([(y + 1) % 4, (y + 3) % 4, (y + 2) % 4, y, 1 - x_hi, x_hi]).astype(jnp.int32)
    down_half, up_quarter = (7, 512, BLK), (7 * BLK, BLK)
    down_sent, up_1, up_3, up_2, g_up, down_kept = call(
        weight_kernel,
        [(down_half, BF16)] + [(up_quarter, BF16)] * 3 + [(up_quarter, F32), (down_half, F32)],
        14 * work,
        (steps, act, dpre, c_4, low_in, back_low, cotangent, got_0, got_1, c_2, c_3, *moved),
    )
    value, far_out, down_sent, up_1, up_3, up_2, g_up, down_kept = lax.optimization_barrier(
        (value, far_out, down_sent, up_1, up_3, up_2, g_up, down_kept)
    )
    got_y1, got_y3 = to_dp(up_1, y_pairs(1)), to_dp(up_3, y_pairs(3))
    got_x = to_dp(down_sent, X_PAIRS)
    got_0 = swap(after(send_0, value), 1)
    fold_out = (fold_out + far_out.astype(F32)).astype(BF16)
    value = halve(value, bits[2], 4)
    value = halve(value, bits[3], 8)
    value, fold_out, got_0 = lax.optimization_barrier((value, fold_out, got_0))
    value = (value + swap(value, 16)).astype(BF16)
    value, got_y1, got_y3 = lax.optimization_barrier((value, got_y1, got_y3))
    got_y2 = to_dp(after(up_2, value), y_pairs(2))
    far_back = swap(after(far_back, value), 24)
    fold_out = swap(after(fold_out, value), 8)
    value = double(value, bits[3], 8)
    value = double(value, bits[2], 4)
    value, got_y2, got_x, far_back, fold_out = lax.optimization_barrier(
        (value, got_y2, got_x, far_back, fold_out)
    )
    fold_back = swap((fold_back + far_back.astype(F32)).astype(BF16), 8)
    down_sent = [
        (part_of(down_kept, (y + step) % 4, 128, 1) + part_of(got_x, (y + step) % 4, 128, 1).astype(F32)).astype(BF16)
        for step in (1, 3, 2)
    ]
    down_kept = part_of(down_kept, y, 128, 1) + part_of(got_x, y, 128, 1).astype(F32)
    down_got = [to_dp(down_sent[0], y_pairs(1)), to_dp(down_sent[1], y_pairs(3))]
    value = double(value, bits[1], 2)
    other = swap(value, 1)
    send_1 = after(send_1, other)
    total, small = call(
        low_terms_kernel, [(pair, F32), ((8, 32, 2 * BLK), BF16)], work,
        (pair_bits, value, other, kept, got_0, down_right, up_left, tokens, cotangent),
    )
    got_1 = swap(send_1, 2)
    small, fold_back, down_got[0], down_got[1], sent_2, send_2 = lax.optimization_barrier(
        (small, fold_back, *down_got, down_sent[2], send_2)
    )
    small = lax.all_to_all(small, "dp", 0, 0, tiled=True)
    got_2 = swap(send_2, 4)
    small, got_2, got_1 = lax.optimization_barrier((small, got_2, got_1))
    small = small.astype(F32).sum(0)
    down_got.append(to_dp(sent_2, y_pairs(2)))
    g_up = g_up + got_y1.astype(F32) + got_y3.astype(F32) + got_y2.astype(F32)
    up_kept = jnp.where(x_hi == 1, g_up[:, 128:], g_up[:, :128])
    up_got = to_dp(jnp.where(x_hi == 1, g_up[:, :128], g_up[:, 128:]).astype(BF16), X_PAIRS)

    def down_sum(begin, end):
        return down_kept[begin:end] + sum(term[begin:end].astype(F32) for term in down_got)

    def up_sum(begin, end):
        cut = slice(begin * BLK, end * BLK)
        return up_kept[cut] + up_got[cut].astype(F32)

    sums = (up_sum(0, 6), down_sum(0, 6), up_sum(6, 7), down_sum(6, 7), small)
    fold_out, fold_back, got_2, total, *sums = lax.optimization_barrier((fold_out, fold_back, got_2, total, *sums))
    output, grad_tokens = call(
        last_kernel, [(block, BF16)] * 2, work // 8, (total, fold_out, fold_back, got_1, got_2)
    )
    return (
        output,
        grad_tokens,
        sums[0].reshape(6, BLK, 128),
        sums[1],
        sums[4][:, :BLK].T,
        sums[2],
        sums[3][0],
        sums[4][:, BLK:],
    )


def solution(mesh):
    placed = (
        P("dp", "tensor"),
        P("dp", "tensor"),
        P(None, None, "tensor"),
        P(None, "tensor", None),
        P("tensor", None),
        P(None, "tensor"),
        P("tensor", None),
        P(None, "tensor"),
        P(),
    )
    return jax.shard_map(
        local,
        mesh=mesh,
        in_specs=placed,
        out_specs=(
            P("dp", "tensor"),
            P("dp", "tensor"),
            P(None, None, ("tensor", "dp")),
            P(None, ("tensor", "dp"), None),
            P("tensor", "dp"),
            P(None, ("tensor", "dp")),
            P(("tensor", "dp"), None),
            P("dp", "tensor"),
        ),
        check_vma=False,
    )
```

```python
import jax
import jax.numpy as jnp
from jax import lax
from jax.experimental import pallas as pl
from jax.experimental.pallas import tpu as pltpu
from jax.sharding import PartitionSpec as P

BLK = 256
F32 = jnp.float32
BF16 = jnp.bfloat16


def swap(value, mask):
    pairs = [(source, source ^ mask) for source in range(lax.axis_size("tensor"))]
    return lax.ppermute(value, "tensor", pairs)


def last_dot(left, right):
    return lax.dot_general(
        left, right, (((1,), (1,)), ((), ())), preferred_element_type=F32
    )


def first_dot(left, right):
    return lax.dot_general(
        left, right, (((0,), (0,)), ((), ())), preferred_element_type=F32
    )


def dot(left, right):
    return jnp.dot(left, right, preferred_element_type=F32)


def after(value, *earlier):
    return lax.optimization_barrier((value, *earlier))[0]


def halve(value, bit, mask):
    low, high = jnp.split(value, 2, 0)
    return jnp.where(bit, high, low) + swap(jnp.where(bit, low, high), mask)


def double(value, bit, mask):
    other = swap(value, mask)
    return jnp.where(
        bit,
        jnp.concatenate([other, value], 0),
        jnp.concatenate([value, other], 0),
    )


def both_halves(value):
    size = lax.axis_size("tensor")
    groups = [list(range(i, i + 4)) for i in range(0, size, 4)]
    return lax.all_gather(value, "tensor", axis_index_groups=groups)


def joined(lows, index):
    return jnp.concatenate([lows[index], lows[index + 2]], 0)


def to_dp(value, pairs):
    return lax.ppermute(value, "dp", pairs)


def y_pairs(step):
    return [(i, (i // 4) * 4 + (i + step) % 4) for i in range(8)]


X_PAIRS = [(i, i ^ 4) for i in range(8)]
VMEM = pl.BlockSpec(memory_space=pltpu.VMEM)
SMEM = pl.BlockSpec(memory_space=pltpu.SMEM)


def call(kernel, outs, flops, args, limit=4):
    shapes = [jax.ShapeDtypeStruct(shape, kind) for shape, kind in outs]
    moved = sum(x.size * x.dtype.itemsize for x in (*args, *shapes))
    return pl.pallas_call(
        kernel,
        out_shape=shapes,
        in_specs=[SMEM if x.dtype == jnp.int32 else VMEM for x in args],
        out_specs=[VMEM] * len(shapes),
        compiler_params=pltpu.CompilerParams(vmem_limit_bytes=limit * 2**20),
        cost_estimate=pl.CostEstimate(
            flops=flops, bytes_accessed=moved, transcendentals=0
        ),
    )(*args)


def quarters(bits, first, second, outs):
    rows = first.shape[0] // 2
    core, near = bits[0] == 1, bits[1] == 1
    mine, other = jnp.where(core, second, first), jnp.where(core, first, second)
    kept, to_core, to_near, to_far = outs
    kept[...] = jnp.where(near, mine[rows:], mine[:rows])
    to_core[...] = jnp.where(near, other[rows:], other[:rows])
    to_near[...] = jnp.where(near, mine[:rows], mine[rows:]).astype(BF16)
    to_far[...] = jnp.where(near, other[:rows], other[rows:]).astype(BF16)


def low_kernel(bits, tokens, cotangent, up_left, down_right, *outs):
    first = dot(tokens[...], up_left[...])
    second = last_dot(cotangent[...], down_right[...])
    quarters(bits, first, second, outs)


def middle_kernel(
    bits, x_0, b_0, b_1, x_2, x_3, x_4, c_0, c_2, c_3, c_4, lows,
    up_0, up_1, up_2, up_3, up_4, up_5, up_right, down, down_left,
    act, dpre, low_in, back_low, kept, fold_out, fold_back, far_out, far_back, send_0, send_1, send_2, *outs,
):
    ups = (up_0, up_1, up_2, up_3, up_4, up_5)
    left, right = slice(0, BLK), slice(BLK, 2 * BLK)
    low_in[...] = joined(lows, 0)
    back_low[...] = joined(lows, 1)
    for j in range(0, 1024, BLK):
        cols = slice(j, j + BLK)
        pre = dot(low_in[...], up_right[:, cols])
        dact = last_dot(back_low[...], down_left[cols, :])
        for k, (x, c) in enumerate((
            (x_0[...], c_0[...]), (b_0[:, left], b_0[:, right]), (b_1[:, left], b_1[:, right]),
            (x_2[...], c_2[...]), (x_3[...], c_3[...]), (x_4[...], c_4[...]),
        )):
            pre = pre + dot(x, ups[k][:, cols])
            dact = dact + last_dot(c, down[k, cols, :])
        value, slope = gelu_both(pre)
        act[:, cols] = value.astype(BF16)
        dpre[:, cols] = (dact * slope).astype(BF16)
    quarters(bits, dot(act[...], down_left[...]), last_dot(dpre[...], up_right[...]), outs)
    for out, back, k in ((far_out, far_back, 5), (fold_out, fold_back, 4)):
        out[...] = dot(act[...], down[k]).astype(out.dtype)
        back[...] = last_dot(dpre[...], ups[k][...]).astype(back.dtype)
    for target, k in ((send_1, 2), (send_2, 3), (send_0, 1), (kept, 0)):
        target[:, left] = dot(act[...], down[k]).astype(target.dtype)
        target[:, right] = last_dot(dpre[...], ups[k][...]).astype(target.dtype)


def weight_kernel(
    steps, act, dpre, c_4, low_in, back_low, c, b_0, b_1, c_2, c_3, m_0, m_1, m_2, m_3, m_4, m_5,
    down_sent, up_1, up_3, up_2, up_kept, down_kept,
):
    cut = slice(BLK, 2 * BLK)
    for n, out in ((4, down_sent), (5, down_kept)):
        left = act[:, pl.ds(pl.multiple_of(steps[n] * 512, 512), 512)]
        rights = (c[...], b_0[:, cut], b_1[:, cut], c_2[...], c_3[...], c_4[...], back_low[...])
        for k, right in enumerate(rights):
            out[k] = first_dot(left, right).astype(out.dtype)
    for n, out in enumerate((up_1, up_3, up_2, up_kept)):
        begin = pl.multiple_of(steps[n] * 128, 128)
        right = jnp.concatenate(
            [dpre[:, pl.ds(begin, 128)], dpre[:, pl.ds(begin + 512, 128)]], 1
        )
        for k, left in enumerate((m_0, m_1, m_2, m_3, m_4, m_5, low_in)):
            out[k * BLK : (k + 1) * BLK] = first_dot(left[...], right).astype(out.dtype)


def low_terms_kernel(bits, mine, other, kept, got_0, down_right, up_left, tokens, cotangent, total, small):
    core = bits[0] == 1
    low_hidden = jnp.where(core, other[...], mine[...])
    back_in = jnp.where(core, mine[...], other[...])
    left = first_dot(back_in, tokens[...]).astype(BF16)
    right = first_dot(low_hidden, cotangent[...]).astype(BF16)
    for n in range(8):
        rows = slice(32 * n, 32 * n + 32)
        small[n, :, :BLK] = left[rows]
        small[n, :, BLK:] = right[rows]
    for cols, term in (
        (slice(0, BLK), dot(low_hidden, down_right[...])),
        (slice(BLK, 2 * BLK), last_dot(back_in, up_left[...])),
    ):
        total[:, cols] = kept[:, cols] + term + got_0[:, cols].astype(F32)


def last_kernel(total, fold_out, fold_back, got_1, got_2, output, grad):
    for target, cols, fold in (
        (output, slice(0, BLK), fold_out),
        (grad, slice(BLK, 2 * BLK), fold_back),
    ):
        terms = [ref[:, cols].astype(F32) for ref in (got_1, got_2)]
        target[...] = (total[:, cols] + fold[...].astype(F32) + terms[0] + terms[1]).astype(BF16)


def part_of(value, index, size, axis):
    return lax.dynamic_slice_in_dim(value, index * size, size, axis)


def gelu_both(pre):
    scale = 0.7978845608028654
    cubic = 0.044715
    square = pre * pre
    inner = jnp.tanh(scale * pre * (1.0 + cubic * square))
    half = 0.5 * (1.0 + inner)
    slope = half + 0.5 * pre * (1.0 - inner * inner) * (
        scale * (1.0 + 3.0 * cubic * square)
    )
    return pre * half, slope


def local(
    tokens,
    cotangent,
    up_blocks,
    down_blocks,
    up_left,
    up_right,
    down_left,
    down_right,
    section_perm,
):
    sections = section_perm.shape[0]
    me = lax.axis_index("tensor")
    dp = lax.axis_index("dp")
    x_hi, y = dp // 4, dp % 4
    bits = [(me >> k) & 1 == 1 for k in range(5)]

    pair_bits = jnp.stack([me & 1, (me >> 1) & 1]).astype(jnp.int32)
    quad = (me >> 2) & 3
    rows = tokens.shape[0]
    work = 2 * rows * BLK * 1024
    wide, pair, block, half = (rows, 1024), (rows, 2 * BLK), (rows, BLK), (rows // 2, BLK)
    part = rows // 8
    split = [(half, F32)] * 2 + [(half, BF16)] * 2

    order = (
        jnp.arange(BLK, dtype=section_perm.dtype)[None, :, None]
        == section_perm[:, None, :]
    ).astype(BF16)
    ups = [
        dot(order[k], up_blocks[k + 1]).astype(BF16) for k in range(sections)
    ]

    x_3 = swap(tokens, 8)
    x_2 = swap(tokens, 4)
    kept, to_core, to_near, to_far = call(
        low_kernel, split, work // 2, (pair_bits, tokens, cotangent, up_left, down_right)
    )
    both = jnp.concatenate([after(tokens, kept), cotangent], 1)
    value = kept + swap(to_core, 1) + swap(to_near, 2).astype(F32) + swap(to_far, 3).astype(F32)
    value, x_3, x_2, both, *ups = lax.optimization_barrier((value, x_3, x_2, both, *ups))
    c_3 = swap(after(cotangent, value), 8)
    x_4 = swap(x_3, 24)
    pieces = [swap(part_of(value, quad ^ d, part, 0), 4 * d) for d in (1, 2, 3)]
    value = part_of(value, quad, part, 0) + sum(pieces)
    value, both = lax.optimization_barrier((value, both))
    got_1 = swap(both, 2)
    got_0 = swap(both, 1)
    value = (value + swap(value, 16)).astype(BF16)
    value, x_4, c_3, got_0, got_1 = lax.optimization_barrier((value, x_4, c_3, got_0, got_1))
    c_4 = swap(c_3, 24)
    c_2 = swap(after(cotangent, value), 4)
    pieces = [value] + [swap(value, 4 * d) for d in (1, 2, 3)]
    ordered = []
    for j in range(4):
        one = [jnp.where(bits[2], pieces[d ^ 1], pieces[d]) for d in range(4)]
        ordered.append(jnp.where(bits[3], one[j ^ 2], one[j]))
    value = jnp.concatenate(ordered, 0)
    lows = both_halves(value)
    x_in = [got_0[:, :BLK], got_1[:, :BLK], x_2, x_3, x_4]
    ups = [up_blocks[0]] + ups
    moved = [tokens] + [dot(x_in[k], order[k]).astype(BF16) for k in range(sections)]
    c_4 = after(c_4, *moved[1:])
    (
        act, dpre, low_in, back_low, kept, fold_out, fold_back, far_out, far_back, send_0, send_1, send_2,
        low_kept, to_core, to_near, to_far,
    ) = call(
        middle_kernel,
        [(wide, BF16)] * 2 + [(block, BF16)] * 2 + [(pair, F32)] + [(block, F32)] * 2 + [(block, BF16)] * 2
        + [(pair, BF16)] * 3 + split,
        28 * work,
        (
            pair_bits, tokens, got_0, got_1, x_2, x_3, x_4, cotangent, c_2, c_3, c_4, lows,
            *ups, up_right, down_blocks, down_left,
        ),
        8,
    )

    from_core = swap(to_core, 1)
    value = low_kept + from_core + swap(to_near, 2).astype(F32) + swap(to_far, 3).astype(F32)
    far_out = swap(far_out, 24)
    steps = jnp.stack([(y + 1) % 4, (y + 3) % 4, (y + 2) % 4, y, 1 - x_hi, x_hi]).astype(jnp.int32)
    down_half, up_quarter = (7, 512, BLK), (7 * BLK, BLK)
    down_sent, up_1, up_3, up_2, g_up, down_kept = call(
        weight_kernel,
        [(down_half, BF16)] + [(up_quarter, BF16)] * 3 + [(up_quarter, F32), (down_half, F32)],
        14 * work,
        (steps, act, dpre, c_4, low_in, back_low, cotangent, got_0, got_1, c_2, c_3, *moved),
    )
    value, far_out, down_sent, up_1, up_3, up_2, g_up, down_kept = lax.optimization_barrier(
        (value, far_out, down_sent, up_1, up_3, up_2, g_up, down_kept)
    )
    got_y1, got_y3 = to_dp(up_1, y_pairs(1)), to_dp(up_3, y_pairs(3))
    got_x = to_dp(down_sent, X_PAIRS)
    got_0 = swap(after(send_0, value), 1)
    fold_out = (fold_out + far_out.astype(F32)).astype(BF16)
    value = halve(value, bits[2], 4)
    value = halve(value, bits[3], 8)
    value, fold_out, got_0 = lax.optimization_barrier((value, fold_out, got_0))
    value = (value + swap(value, 16)).astype(BF16)
    value, got_y1, got_y3 = lax.optimization_barrier((value, got_y1, got_y3))
    got_y2 = to_dp(after(up_2, value), y_pairs(2))
    far_back = swap(after(far_back, value), 24)
    fold_out = swap(after(fold_out, value), 8)
    value = double(value, bits[3], 8)
    value = double(value, bits[2], 4)
    value, got_y2, got_x, far_back, fold_out = lax.optimization_barrier(
        (value, got_y2, got_x, far_back, fold_out)
    )
    fold_back = swap((fold_back + far_back.astype(F32)).astype(BF16), 8)
    down_sent = [
        (part_of(down_kept, (y + step) % 4, 128, 1) + part_of(got_x, (y + step) % 4, 128, 1).astype(F32)).astype(BF16)
        for step in (1, 3, 2)
    ]
    down_kept = part_of(down_kept, y, 128, 1) + part_of(got_x, y, 128, 1).astype(F32)
    down_got = [to_dp(down_sent[0], y_pairs(1)), to_dp(down_sent[1], y_pairs(3))]
    value = double(value, bits[1], 2)
    other = swap(value, 1)
    send_1 = after(send_1, other)
    total, small = call(
        low_terms_kernel, [(pair, F32), ((8, 32, 2 * BLK), BF16)], work,
        (pair_bits, value, other, kept, got_0, down_right, up_left, tokens, cotangent),
    )
    got_1 = swap(send_1, 2)
    _, fold_back, down_got[0], down_got[1], sent_2, send_2 = lax.optimization_barrier(
        (small, fold_back, *down_got, down_sent[2], send_2)
    )
    small = lax.all_to_all(small, "dp", 0, 0, tiled=True)
    got_2 = swap(send_2, 4)
    small, got_2, got_1 = lax.optimization_barrier((small, got_2, got_1))
    small = small.astype(F32).sum(0)
    down_got.append(to_dp(sent_2, y_pairs(2)))
    g_up = g_up + got_y1.astype(F32) + got_y3.astype(F32) + got_y2.astype(F32)
    up_kept = jnp.where(x_hi == 1, g_up[:, 128:], g_up[:, :128])
    up_got = to_dp(jnp.where(x_hi == 1, g_up[:, :128], g_up[:, 128:]).astype(BF16), X_PAIRS)

    def down_sum(begin, end):
        return down_kept[begin:end] + sum(term[begin:end].astype(F32) for term in down_got)

    def up_sum(begin, end):
        cut = slice(begin * BLK, end * BLK)
        return up_kept[cut] + up_got[cut].astype(F32)

    sums = (up_sum(0, 6), down_sum(0, 6), up_sum(6, 7), down_sum(6, 7), small)
    fold_out, fold_back, got_2, total, *sums = lax.optimization_barrier((fold_out, fold_back, got_2, total, *sums))
    output, grad_tokens = call(
        last_kernel, [(block, BF16)] * 2, work // 8, (total, fold_out, fold_back, got_1, got_2)
    )
    return (
        output,
        grad_tokens,
        sums[0].reshape(6, BLK, 128),
        sums[1],
        sums[4][:, :BLK].T,
        sums[2],
        sums[3][0],
        sums[4][:, BLK:],
    )


def solution(mesh):
    placed = (
        P("dp", "tensor"),
        P("dp", "tensor"),
        P(None, None, "tensor"),
        P(None, "tensor", None),
        P("tensor", None),
        P(None, "tensor"),
        P("tensor", None),
        P(None, "tensor"),
        P(),
    )
    return jax.shard_map(
        local,
        mesh=mesh,
        in_specs=placed,
        out_specs=(
            P("dp", "tensor"),
            P("dp", "tensor"),
            P(None, None, ("tensor", "dp")),
            P(None, ("tensor", "dp"), None),
            P("tensor", "dp"),
            P(None, ("tensor", "dp")),
            P(("tensor", "dp"), None),
            P("dp", "tensor"),
        ),
        check_vma=False,
    )
```
